512 devices in a mesh: row: 16 (over x, z_lo), col: 32 (over z_hi, y, core).
Axes of the slice: x: 4, y: 8, z: 8 (z_hi: 2, z_lo: 4; z = z_hi * 4 + z_lo), core: 2. Of those that a mesh axis runs over, the one named last changes fastest.
Arguments:
- integrals: float32 [16, 256, 32, 256], P('row', None, 'col'), may hold values from -0.0625 to 0.0625
- amplitudes: float32 [32, 256, 16, 256], P('row', 'col'), may hold values from -6 to 6
Outputs:
- cycle: float32 [4096, 4096], P('row', 'col')
The draws below stay inside these ranges and needn't reach their ends.
All inputs are finite; a program needn't handle non-finite values.
Results may differ from the reference program's by a relative error of at most 0.00007.
Values sent between devices are 32-bit elements; how exact they have to be, the bound alone decides.
A program may use at most 64 MiB of HBM per device.

```python
import jax
import jax.numpy as jnp
from jax import lax

OCC = 32
VIRT = 256
OCC_BLOCK = 16
KDIM = 8192
NDIM = 4096


def levels(key, shape, split, least, high):
    level = 1.0
    for dim, parts in split:
        steps = jax.random.uniform(jax.random.fold_in(jax.random.fold_in(key, 6), dim), (parts,), jnp.float32, least / len(split), high / len(split))
        level = level * jnp.repeat(jnp.exp(steps), shape[dim] // parts).reshape((-1,) + (1,) * (len(shape) - 1 - dim))
    return level


def scatter_about(own_key, shape, spread, reach, cuts=(), held_as=jnp.bfloat16):
    factor_of = levels(own_key, shape, cuts, -0.22, 0.18) if cuts else 1.0
    array = jax.random.normal(own_key, shape, jnp.float32) * spread * factor_of
    return jnp.minimum(jnp.maximum(array, -reach), reach).astype(held_as)


def setup_inputs(seed: int = 0) -> dict:
    arg_keys = jax.random.split(jax.random.key(seed), 3)
    integrals = scatter_about(arg_keys[0], (OCC_BLOCK, VIRT, OCC, VIRT), KDIM ** -0.5, 0.0625, ((0, 16), (2, 32)), jnp.float32)
    amplitudes = scatter_about(arg_keys[1], (OCC, VIRT, OCC_BLOCK, VIRT), 1.0, 6.0, ((0, 16), (1, 32)), jnp.float32)
    return dict(integrals=integrals, amplitudes=amplitudes)


def reference(integrals, amplitudes):
    left = integrals.reshape(NDIM, KDIM)
    right = amplitudes.reshape(KDIM, NDIM)
    cycle_part = jnp.dot(left, right, precision=lax.Precision.HIGHEST, preferred_element_type=jnp.float32)
    return cycle_part + cycle_part.T
```

```python
import jax
import jax.numpy as jnp
from jax import lax
from jax.experimental import pallas as pl
from jax.experimental.pallas import tpu as pltpu
from jax.sharding import PartitionSpec as P

MESH = pl.DeviceIdType.MESH
RING = 8
F32, BF16 = jnp.float32, jnp.bfloat16


def device(x, z, y, core):
    return (x * 4 + z % 4, (z // 4) * 16 + y * 2 + core)


def split(value):
    high = value.astype(BF16)
    return high, (value - high.astype(F32)).astype(BF16)


def kernel(
    left_ref, right_ref, out_ref,
    pieces, left_all, right_all, left_hi, left_lo, right_hi, right_lo,
    partial, arrived, summed, own, mirror,
    spread_send, spread_recv, move_send, move_recv,
    ysend, yrecv, zsend, zrecv, share_send, share_recv,
    part_send, part_recv, own_send, own_recv, mirror_send, mirror_recv,
):
    row, col = lax.axis_index("row"), lax.axis_index("col")
    x, zl, zh, y, core = row // 4, row % 4, col // 16, (col // 2) % 8, col % 2
    z = zh * 4 + zl
    x1, x0, zl1, zl0 = x // 2, x % 2, zl // 2, zl % 2
    y2, y1, y0 = y // 4, (y // 2) % 2, y % 2

    spread_x, spread_z = x1 * 2 + zl0, zh * 4 + zl1 * 2 + x0
    spread_home = x0 == zl0
    move_to = (zh * 2 + y0, x0 * 4 + zl, y2 * 4 + y1 * 2 + x1)
    move_from = (y0 * 2 + zh, x1 * 4 + zl, y2 * 4 + y1 * 2 + x0)
    move_home = (x1 == x0) & (x0 == zh) & (zh == y0)
    own_to = (x1 * 2 + zh, x0 * 4 + zl, y)
    own_home = x0 == zh
    mirror_to = (2 * x0 + y2, x1 * 4 + y % 4, 4 * zh + zl)
    mirror_from = (2 * zh + x1, y2 * 4 + y % 4, 4 * x0 + zl)
    mirror_home = (mirror_to[0] == x) & (mirror_to[1] == z) & (mirror_to[2] == y)

    yr, yl, zr, zlft = (y + 1) % RING, (y + 7) % RING, (z + 1) % RING, (z + 7) % RING

    barrier = pltpu.get_barrier_semaphore()

    def greet(target):
        pl.semaphore_signal(barrier, inc=1, device_id=target, device_id_type=MESH)

    greet(device(x, z, yr, core))
    greet(device(x, z, yl, core))
    greet(device(x, zr, y, core))
    greet(device(x, zlft, y, core))
    greet(device(x, z, y, 1 - core))
    for dx in range(1, 4):
        greet(device((x + dx) % 4, z, y, core))
    for dy in range(8):
        for de in range(2):
            target = device(spread_x, spread_z, (y + dy) % 8, (core + de) % 2)
            if dy == 0 and de == 0:
                @pl.when(jnp.logical_not(spread_home))
                def _():
                    greet(target)
            else:
                greet(target)

    @pl.when(jnp.logical_not(move_home))
    def _():
        greet(device(*move_from, core))

    for k in range(2):
        for high in range(2):
            for e in range(2):
                block = right_ref[k, :, 8 * high : 8 * high + 8, 128 * e : 128 * e + 128]
                block = jnp.swapaxes(block, 0, 1)
                for j in range(8):
                    pieces[j, e, k, :, 128 * high : 128 * high + 128] = block[j]

    away = jnp.logical_not(move_home).astype(jnp.int32) + jnp.logical_not(spread_home).astype(jnp.int32)
    pl.semaphore_wait(barrier, 23 + away)

    sends = []

    def copy(src, dst, send_sem, recv_sem, target):
        return pltpu.make_async_remote_copy(
            src_ref=src, dst_ref=dst, send_sem=send_sem, recv_sem=recv_sem,
            device_id=target, device_id_type=MESH,
        )

    def start(*args):
        made = copy(*args)
        made.start()
        sends.append(made)

    def arrive(ref, sem):
        pltpu.make_async_copy(ref, ref, sem).wait()

    for dy in (0, 1, 7, 2, 6, 3, 5, 4):
        for de in range(2):
            ty, te = (y + dy) % 8, (core + de) % 2
            src = pieces.at[ty, te]
            place = pl.ds(pl.multiple_of(16 * y + 8 * core, 8), 8)
            dst = right_all.at[spread_z, :, place, :]
            made = copy(src, dst, spread_send.at[dy * 2 + de], spread_recv, device(spread_x, spread_z, ty, te))
            if dy == 0 and de == 0:
                @pl.when(spread_home)
                def _():
                    pltpu.make_async_copy(src, dst, spread_recv).start()

                @pl.when(jnp.logical_not(spread_home))
                def _():
                    made.start()
            else:
                made.start()
                sends.append(made)
            if dy == 0 and de == 0:
                first = made

    moves = []
    for h in range(2):
        src = left_ref.at[pl.ds(128 * h, 128)]
        dst = left_all.at[move_to[2], core, h]
        made = copy(src, dst, move_send.at[h], move_recv.at[h], device(*move_to, core))
        moves.append(made)

        @pl.when(move_home)
        def _():
            pltpu.make_async_copy(src, dst, move_recv.at[h]).start()

        @pl.when(jnp.logical_not(move_home))
        def _():
            made.start()

    def send_y(slot, h, way, step):
        ref = left_all.at[slot, core, h]
        start(ref, ref, ysend.at[way, step, h], yrecv.at[way, step, h], device(x, z, yr if way == 0 else yl, core))

    def send_z(slot, h, way, step):
        ref = right_all.at[slot, h]
        start(ref, ref, zsend.at[way, step, h], zrecv.at[way, step, h], device(x, zr if way == 0 else zlft, y, core))

    def share(slot, h, number):
        ref = left_all.at[slot, core, h]
        start(ref, ref, share_send.at[number], share_recv.at[number], device(x, z, y, 1 - core))

    def split_left(slot, e, h):
        left_hi[slot, e, h], left_lo[slot, e, h] = split(left_all[slot, e, h])

    def split_right(slot, k):
        part = slot // 4
        kind = (slot % 2) * 2 + (slot // 2) % 2
        half = pl.ds(pl.multiple_of(128 * part, 128), 128)
        right_hi[kind, k, half, :], right_lo[kind, k, half, :] = split(right_all[slot, k])

    arrive(right_all.at[z], spread_recv)
    for i in range(2):
        send_z(z, i, 0, 0)
        send_z(z, 1 - i, 1, 0)
    for h in range(2):
        arrive(left_all.at[y, core, h], move_recv.at[h])
        send_y(y, h, 0, 0)
        send_y(y, h, 1, 0)
        share(y, h, h)
    for k in range(2):
        split_right(z, k)
    for h in range(2):
        split_left(y, core, h)
    shared = [(y, 0), (y, 1)]
    for step in range(4):
        for i in range(2):
            for way in range(2):
                h = i if way == 0 else 1 - i
                if step == 3 and i == 1:
                    continue
                last = step == 3 or (step == 2 and i == 1)
                slot = (z - 1 - step + 8) % 8 if way == 0 else (z + 1 + step) % 8
                arrive(right_all.at[slot, h], zrecv.at[way, step, h])
                if not last:
                    send_z(slot, h, way, step + 1)
                slot_y = (y - 1 - step + 8) % 8 if way == 0 else (y + 1 + step) % 8
                arrive(left_all.at[slot_y, core, h], yrecv.at[way, step, h])
                if not last:
                    send_y(slot_y, h, way, step + 1)
                share(slot_y, h, len(shared))
                shared.append((slot_y, h))
                split_right(slot, h)
                split_left(slot_y, core, h)
    for number, (slot_y, h) in enumerate(shared):
        arrive(left_all.at[slot_y, 1 - core, h], share_recv.at[number])
        split_left(slot_y, 1 - core, h)

    parts = []
    for h in range(2):
        for f in range(2):
            total = jnp.zeros((128, 256), F32)
            for kind in range(4):
                slot_y = (kind // 2) * 4 + (kind % 2) * 2 + f
                for e in range(2):
                    lh, ll = left_hi[slot_y, e, h], left_lo[slot_y, e, h]
                    rh, rl = right_hi[kind, e], right_lo[kind, e]
                    total += jnp.dot(lh, rh, preferred_element_type=F32)
                    total += jnp.dot(lh, rl, preferred_element_type=F32)
                    total += jnp.dot(ll, rh, preferred_element_type=F32)
            partial[2 * f, h] = total[:, :128]
            partial[2 * f + 1, h] = total[:, 128:]
        for dx in range(1, 4):
            tx = (x + dx) % 4
            start(partial.at[tx, h], arrived.at[dx - 1, h], part_send.at[dx - 1, h], part_recv.at[dx - 1, h],
                  device(tx, z, y, core))

    owns = []
    for h in range(2):
        for d in range(3):
            arrive(arrived.at[d, h], part_recv.at[d, h])
        summed[h] = partial[x, h] + arrived[0, h] + arrived[1, h] + arrived[2, h]
        made_own = copy(summed.at[h], own.at[h], own_send.at[h], own_recv.at[h], device(*own_to, core))
        made_mirror = copy(summed.at[h], mirror.at[core], mirror_send.at[h], mirror_recv.at[core],
                           device(*mirror_to, h))
        at_home = mirror_home & (core == h)
        owns.append((made_own, made_mirror, at_home))

        @pl.when(own_home)
        def _():
            pltpu.make_async_copy(summed.at[h], own.at[h], own_recv.at[h]).start()

        @pl.when(jnp.logical_not(own_home))
        def _():
            made_own.start()

        @pl.when(at_home)
        def _():
            pltpu.make_async_copy(summed.at[h], mirror.at[core], mirror_recv.at[core]).start()

        @pl.when(jnp.logical_not(at_home))
        def _():
            made_mirror.start()

    for h in range(2):
        arrive(own.at[h], own_recv.at[h])
    for e in range(2):
        arrive(mirror.at[e], mirror_recv.at[e])
        out_ref[128 * e : 128 * e + 128, :] = own[e] + jnp.transpose(mirror[e])

    for made in sends:
        made.wait_send()

    @pl.when(jnp.logical_not(spread_home))
    def _():
        first.wait_send()

    for h in range(2):
        @pl.when(jnp.logical_not(move_home))
        def _():
            moves[h].wait_send()

        made_own, made_mirror, at_home = owns[h]

        @pl.when(jnp.logical_not(own_home))
        def _():
            made_own.wait_send()

        @pl.when(jnp.logical_not(at_home))
        def _():
            made_mirror.wait_send()


def body(integrals, amplitudes):
    dma = pltpu.SemaphoreType.DMA
    return pl.pallas_call(
        kernel,
        out_shape=jax.ShapeDtypeStruct((256, 128), F32),
        in_specs=[pl.BlockSpec(memory_space=pl.ANY), pl.BlockSpec(memory_space=pltpu.VMEM)],
        out_specs=pl.BlockSpec(memory_space=pltpu.VMEM),
        scratch_shapes=[
            pltpu.VMEM((8, 2, 2, 8, 256), F32),
            pltpu.VMEM((8, 2, 2, 128, 256), F32),
            pltpu.VMEM((8, 2, 128, 256), F32),
            pltpu.VMEM((8, 2, 2, 128, 256), BF16),
            pltpu.VMEM((8, 2, 2, 128, 256), BF16),
            pltpu.VMEM((4, 2, 256, 256), BF16),
            pltpu.VMEM((4, 2, 256, 256), BF16),
            pltpu.VMEM((4, 2, 128, 128), F32),
            pltpu.VMEM((3, 2, 128, 128), F32),
            pltpu.VMEM((2, 128, 128), F32),
            pltpu.VMEM((2, 128, 128), F32),
            pltpu.VMEM((2, 128, 128), F32),
            dma((16,)), dma,
            dma((2,)), dma((2,)),
            dma((2, 4, 2)), dma((2, 4, 2)),
            dma((2, 4, 2)), dma((2, 4, 2)),
            dma((16,)), dma((16,)),
            dma((3, 2)), dma((3, 2)),
            dma((2,)), dma((2,)),
            dma((2,)), dma((2,)),
        ],
        compiler_params=pltpu.CompilerParams(
            collective_id=0, has_side_effects=True, vmem_limit_bytes=40 << 20
        ),
        cost_estimate=pl.CostEstimate(flops=3 * 2**29, bytes_accessed=1 << 20, transcendentals=0),
        name="cycle",
    )(integrals.reshape(256, 256), amplitudes)


def solution(mesh):
    return jax.shard_map(
        body,
        mesh=mesh,
        in_specs=(P("row", None, "col", None), P("row", "col", None, None)),
        out_specs=P("row", "col"),
        check_vma=False,
    )
```

```python
import jax
import jax.numpy as jnp
from jax import lax
from jax.experimental import pallas as pl
from jax.experimental.pallas import tpu as pltpu
from jax.sharding import PartitionSpec as P

MESH = pl.DeviceIdType.MESH
RING = 8
F32, BF16 = jnp.float32, jnp.bfloat16


def device(x, z, y, core):
    return (x * 4 + z % 4, (z // 4) * 16 + y * 2 + core)


def split(value):
    high = value.astype(BF16)
    return high, (value - high.astype(F32)).astype(BF16)


def dot(first, second):
    return jnp.dot(first, second, preferred_element_type=F32)


def kernel(
    left_ref, right_ref, out_ref,
    packed, stage, far, left_all, pieces, rows_here, right_all, left_hi, left_lo, right_hi, right_lo,
    partial, arrived, summed, own, mirror,
    pack_send, pack_recv, far_send, far_recv, spread_send, spread_recv, third_send, third_recv,
    ysend, yrecv, zsend, zrecv, share_send, share_recv,
    part_send, part_recv, own_send, own_recv, mirror_send, mirror_recv,
):
    row, col = lax.axis_index("row"), lax.axis_index("col")
    x, zl, zh, y, core = row // 4, row % 4, col // 16, (col // 2) % 8, col % 2
    z = zh * 4 + zl
    x1, x0 = x // 2, x % 2

    barrier = pltpu.get_barrier_semaphore()

    def greet(*target):
        pl.semaphore_signal(barrier, inc=1, device_id=device(*target), device_id_type=MESH)

    for dx in range(1, 4):
        greet((x + dx) % 4, z, y, core)
    for dz in (1, 7, 4):
        greet(x, (z + dz) % 8, y, core)
    for dy in range(8):
        for de in range(2):
            if dy or de:
                greet(x, z, (y + dy) % 8, (core + de) % 2)

    for half in range(2):
        for k in range(2):
            for e in range(2):
                block = right_ref[k, :, 8 * half : 8 * half + 8, 128 * e : 128 * e + 128]
                block = jnp.swapaxes(block, 0, 1)
                for j in range(8):
                    pieces[half, j, e, k] = block[j]

    c = lax.broadcasted_iota(jnp.int32, (256, 512), 0)
    t = lax.broadcasted_iota(jnp.int32, (256, 512), 1)
    place = (c // 32) % 4 * 128 + c // 128 * 32 + c % 32
    pick = [(t == place + shift).astype(F32).astype(BF16) for shift in (0, 64)]
    quarters = jnp.zeros((128, 512), F32)
    for i in range(2):
        begin = pl.multiple_of(128 * (zh if i == 0 else 1 - zh), 128)
        high, low = split(left_ref[pl.ds(begin, 128), :])
        quarters += dot(high, pick[i]) + dot(low, pick[i])
    for q in range(4):
        packed[q] = quarters[:, 128 * q : 128 * q + 128]

    pl.semaphore_wait(barrier, 21)

    sends = []
    maybe = []

    def copy(src, dst, send_sem, recv_sem, target):
        return pltpu.make_async_remote_copy(
            src_ref=src, dst_ref=dst, send_sem=send_sem, recv_sem=recv_sem,
            device_id=device(*target), device_id_type=MESH,
        )

    def start(*args):
        made = copy(*args)
        made.start()
        sends.append(made)

    def start_or_keep(home, src, dst, send_sem, recv_sem, target):
        made = copy(src, dst, send_sem, recv_sem, target)

        @pl.when(home)
        def _():
            pltpu.make_async_copy(src, dst, recv_sem).start()

        @pl.when(jnp.logical_not(home))
        def _():
            made.start()

        maybe.append((home, made))

    def arrive(ref, sem):
        pltpu.make_async_copy(ref, ref, sem).wait()

    def spread(half):
        mine = pl.ds(pl.multiple_of(16 * y + 8 * core, 8), 8)
        dst = rows_here.at[half, :, mine, :]
        for dy in (1, 7, 2, 6, 3, 5, 4, 0):
            for de in range(2):
                ty, te = (y + dy) % 8, (core + de) % 2
                src = pieces.at[half, ty, te]
                if dy or de:
                    start(src, dst, spread_send.at[half, dy * 2 + de], spread_recv.at[half], (x, z, ty, te))
                else:
                    pltpu.make_async_copy(src, dst, spread_recv.at[half]).start()

    def spread_x(half):
        for dx in range(4):
            tx = (x + dx) % 4
            src = rows_here.at[half, :, pl.ds(pl.multiple_of(32 * tx, 32), 32), :]
            dst = right_all.at[z, half, x]
            if dx:
                start(src, dst, third_send.at[half, dx], third_recv.at[half], (tx, z, y, core))
            else:
                pltpu.make_async_copy(src, dst, third_recv.at[half]).start()

    spread(0)
    goes = (x1 != zh).astype(jnp.int32)
    for dx in range(4):
        tx = (x + dx) % 4
        dst = stage.at[goes, x0]
        if dx:
            start(packed.at[tx], dst, pack_send.at[dx], pack_recv.at[goes], (tx, z, y, core))
        else:
            pltpu.make_async_copy(packed.at[tx], dst, pack_recv.at[goes]).start()
    spread(1)
    arrive(stage.at[1], pack_recv.at[1])
    start(stage.at[1], far, far_send, far_recv, (x, (z + 4) % 8, y, core))
    arrive(rows_here.at[0], spread_recv.at[0])
    spread_x(0)
    arrive(rows_here.at[1], spread_recv.at[1])
    spread_x(1)

    yr, yl, zr, zlft = (y + 1) % RING, (y + 7) % RING, (z + 1) % RING, (z + 7) % RING

    def send_y(slot, h, way, step):
        ref = left_all.at[slot, core, h]
        start(ref, ref, ysend.at[way, step, h], yrecv.at[way, step, h], (x, z, yr if way == 0 else yl, core))

    def send_z(slot, h, way, step):
        ref = right_all.at[slot, h]
        start(ref, ref, zsend.at[way, step, h], zrecv.at[way, step, h], (x, zr if way == 0 else zlft, y, core))

    def share(slot, h, number):
        ref = left_all.at[slot, core, h]
        start(ref, ref, share_send.at[number], share_recv.at[number], (x, z, y, 1 - core))

    def split_left(slot, e, h):
        lanes = pl.ds(pl.multiple_of(128 * e, 128), 128)
        left_hi[slot, h, :, lanes], left_lo[slot, h, :, lanes] = split(left_all[slot, e, h])

    def split_right(slot, half):
        high, low = split(right_all[slot, half])
        for s3 in range(2):
            for s2 in range(2):
                for k in range(2):
                    begin = pl.multiple_of(128 * k + 64 * s3 + 32 * (slot // 4), 32)
                    at = (s2 * 4 + slot % 4, pl.ds(begin, 32), slice(128 * half, 128 * half + 128))
                    right_hi[at] = high[2 * s3 + s2, k]
                    right_lo[at] = low[2 * s3 + s2, k]

    def ring_z_begin(h):
        arrive(right_all.at[z, h], third_recv.at[h])
        send_z(z, h, h, 0)
        send_z(z, h, 1 - h, 0)

    ring_z_begin(0)
    arrive(stage.at[0], pack_recv.at[0])
    arrive(far, far_recv)
    low_lane = lax.broadcasted_iota(jnp.int32, (128, 128), 1) < 64
    for f in range(2):
        near_part, far_part = stage[0, f], far[f]
        even = jnp.where(zh == 0, near_part, far_part)
        odd = jnp.where(zh == 0, far_part, near_part)
        left_all[y, core, f, 0:128] = jnp.where(low_lane, even, odd)
        left_all[y, core, f, 128:256] = pltpu.roll(jnp.where(low_lane, odd, even), 64, 1)
        send_y(y, f, f, 0)
        send_y(y, f, 1 - f, 0)
        share(y, f, f)
    ring_z_begin(1)
    shared = [(y, 0), (y, 1)]
    for h in range(2):
        split_right(z, h)
        split_left(y, core, h)
    for step in range(4):
        for i in range(2):
            for way in range(2):
                h = i if way == 0 else 1 - i
                if step == 3 and i == 1:
                    continue
                last = step == 3 or (step == 2 and i == 1)
                slot = (z - 1 - step + 8) % 8 if way == 0 else (z + 1 + step) % 8
                arrive(right_all.at[slot, h], zrecv.at[way, step, h])
                if not last:
                    send_z(slot, h, way, step + 1)
                slot_y = (y - 1 - step + 8) % 8 if way == 0 else (y + 1 + step) % 8
                arrive(left_all.at[slot_y, core, h], yrecv.at[way, step, h])
                if not last:
                    send_y(slot_y, h, way, step + 1)
                share(slot_y, h, len(shared))
                shared.append((slot_y, h))
                split_right(slot, h)
                split_left(slot_y, core, h)
    for number, (slot_y, h) in enumerate(shared):
        arrive(left_all.at[slot_y, 1 - core, h], share_recv.at[number])
        split_left(slot_y, 1 - core, h)

    for f in range(2):
        total = jnp.zeros((256, 256), F32)
        for unit in range(8):
            lh, ll, rh, rl = left_hi[unit, f], left_lo[unit, f], right_hi[unit], right_lo[unit]
            total += dot(lh, rh) + dot(lh, rl) + dot(ll, rh)
        for half in range(2):
            partial[f, half] = total[:, 128 * half : 128 * half + 128]
        for dx in range(1, 4):
            tx = (x + dx) % 4
            src = partial.at[f, :, pl.ds(pl.multiple_of(64 * tx, 64), 64), :]
            start(src, arrived.at[dx - 1, f], part_send.at[dx - 1, f], part_recv.at[dx - 1, f], (tx, z, y, core))

    for f in range(2):
        for d in range(3):
            arrive(arrived.at[d, f], part_recv.at[d, f])
        kept = partial[f, :, pl.ds(pl.multiple_of(64 * x, 64), 64), :]
        summed[f] = kept + arrived[0, f] + arrived[1, f] + arrived[2, f]
        for half in range(2):
            src = summed.at[f, half]
            to = (2 * half + y // 4, zh * 4 + y % 4, 4 * f + zl, x // 2)
            dst = mirror.at[core, pl.ds(pl.multiple_of(64 * x0, 64), 64)]
            home = (to[0] == x) & (to[1] == z) & (to[2] == y) & (to[3] == core)
            start_or_keep(home, src, dst, mirror_send.at[f, half], mirror_recv, to)
            to = (2 * zh + f, half * 4 + zl, y, core)
            dst = own.at[pl.ds(pl.multiple_of(64 * x, 64), 64)]
            home = (to[0] == x) & (to[1] == z)
            start_or_keep(home, src, dst, own_send.at[f, half], own_recv, to)

    arrive(own, own_recv)
    arrive(mirror, mirror_recv)
    for e in range(2):
        out_ref[128 * e : 128 * e + 128, :] = own[128 * e : 128 * e + 128] + jnp.transpose(mirror[e])

    for made in sends:
        made.wait_send()
    for home, made in maybe:
        pl.when(jnp.logical_not(home))(made.wait_send)


def body(integrals, amplitudes):
    dma = pltpu.SemaphoreType.DMA
    return pl.pallas_call(
        kernel,
        out_shape=jax.ShapeDtypeStruct((256, 128), F32),
        in_specs=[pl.BlockSpec(memory_space=pltpu.VMEM), pl.BlockSpec(memory_space=pltpu.VMEM)],
        out_specs=pl.BlockSpec(memory_space=pltpu.VMEM),
        scratch_shapes=[
            pltpu.VMEM((4, 128, 128), F32),
            pltpu.VMEM((2, 2, 128, 128), F32),
            pltpu.VMEM((2, 128, 128), F32),
            pltpu.VMEM((8, 2, 2, 256, 128), F32),
            pltpu.VMEM((2, 8, 2, 2, 8, 128), F32),
            pltpu.VMEM((2, 2, 128, 128), F32),
            pltpu.VMEM((8, 2, 4, 2, 32, 128), F32),
            pltpu.VMEM((8, 2, 256, 256), BF16),
            pltpu.VMEM((8, 2, 256, 256), BF16),
            pltpu.VMEM((8, 256, 256), BF16),
            pltpu.VMEM((8, 256, 256), BF16),
            pltpu.VMEM((2, 2, 256, 128), F32),
            pltpu.VMEM((3, 2, 2, 64, 128), F32),
            pltpu.VMEM((2, 2, 64, 128), F32),
            pltpu.VMEM((256, 128), F32),
            pltpu.VMEM((2, 128, 128), F32),
            dma((4,)), dma((2,)),
            dma, dma,
            dma((2, 16)), dma((2,)),
            dma((2, 4)), dma((2,)),
            dma((2, 4, 2)), dma((2, 4, 2)),
            dma((2, 4, 2)), dma((2, 4, 2)),
            dma((16,)), dma((16,)),
            dma((3, 2)), dma((3, 2)),
            dma((2, 2)), dma,
            dma((2, 2)), dma,
        ],
        compiler_params=pltpu.CompilerParams(
            collective_id=0, has_side_effects=True, vmem_limit_bytes=40 << 20
        ),
        cost_estimate=pl.CostEstimate(flops=3 * 2**29, bytes_accessed=1 << 20, transcendentals=0),
        name="cycle",
    )(integrals.reshape(256, 256), amplitudes)


def solution(mesh):
    return jax.shard_map(
        body,
        mesh=mesh,
        in_specs=(P("row", None, "col", None), P("row", "col", None, None)),
        out_specs=P("row", "col"),
        check_vma=False,
    )
```

```python
import jax
import jax.numpy as jnp
from jax import lax
from jax.experimental import pallas as pl
from jax.experimental.pallas import tpu as pltpu
from jax.sharding import PartitionSpec as P

MESH = pl.DeviceIdType.MESH
RING = 8
F32, BF16 = jnp.float32, jnp.bfloat16


def device(x, z, y, core):
    return (x * 4 + z % 4, (z // 4) * 16 + y * 2 + core)


def split(value):
    high = value.astype(BF16)
    return high, (value - high.astype(F32)).astype(BF16)


def dot(first, second):
    return jnp.dot(first, second, preferred_element_type=F32)


def kernel(
    left_ref, right_ref, out_ref,
    packed, stage, far, left_all, pieces, rows_here, right_all, left_hi, left_lo, right_hi, right_lo,
    partial, arrived, summed, own, mirror,
    pack_send, pack_recv, far_send, far_recv, spread_send, spread_recv, third_send, third_recv,
    ysend, yrecv, zsend, zrecv, share_send, share_recv,
    part_send, part_recv, own_send, own_recv, mirror_send, mirror_recv,
):
    row, col = lax.axis_index("row"), lax.axis_index("col")
    x, zl, zh, y, core = row // 4, row % 4, col // 16, (col // 2) % 8, col % 2
    z = zh * 4 + zl
    x1, x0 = x // 2, x % 2

    barrier = pltpu.get_barrier_semaphore()

    def greet(*target):
        pl.semaphore_signal(barrier, inc=1, device_id=device(*target), device_id_type=MESH)

    for dx in range(1, 4):
        greet((x + dx) % 4, z, y, core)
    for dz in (1, 7, 4):
        greet(x, (z + dz) % 8, y, core)
    for dy in range(8):
        for de in range(2):
            if dy or de:
                greet(x, z, (y + dy) % 8, (core + de) % 2)

    for half in range(2):
        for k in range(2):
            for e in range(2):
                block = right_ref[k, :, 8 * half : 8 * half + 8, 128 * e : 128 * e + 128]
                block = jnp.swapaxes(block, 0, 1)
                for j in range(8):
                    pieces[half, j, e, k] = block[j]

    c = lax.broadcasted_iota(jnp.int32, (256, 512), 0)
    t = lax.broadcasted_iota(jnp.int32, (256, 512), 1)
    place = (c // 32) % 4 * 128 + c // 128 * 32 + c % 32
    quarters = jnp.zeros((128, 512), F32)
    for i in range(2):
        pick = (t == place + 64 * i).astype(F32).astype(BF16)
        for lanes in range(2):
            begin = 256 * (zh if i == 0 else 1 - zh) + lanes
            high, low = split(left_ref[pl.ds(begin, 128, stride=2), :])
            chosen = pick[128 * lanes : 128 * lanes + 128]
            quarters += dot(high, chosen) + dot(low, chosen)
    for q in range(4):
        packed[q] = quarters[:, 128 * q : 128 * q + 128]

    pl.semaphore_wait(barrier, 21)

    sends = []
    maybe = []

    def copy(src, dst, send_sem, recv_sem, target):
        return pltpu.make_async_remote_copy(
            src_ref=src, dst_ref=dst, send_sem=send_sem, recv_sem=recv_sem,
            device_id=device(*target), device_id_type=MESH,
        )

    def start(*args):
        made = copy(*args)
        made.start()
        sends.append(made)

    def start_or_keep(home, src, dst, send_sem, recv_sem, target):
        made = copy(src, dst, send_sem, recv_sem, target)

        @pl.when(home)
        def _():
            pltpu.make_async_copy(src, dst, recv_sem).start()

        @pl.when(jnp.logical_not(home))
        def _():
            made.start()

        maybe.append((home, made))

    def arrive(ref, sem):
        pltpu.make_async_copy(ref, ref, sem).wait()

    def spread(half):
        mine = pl.ds(pl.multiple_of(16 * y + 8 * core, 8), 8)
        dst = rows_here.at[half, :, mine, :]
        for dy in (4, 3, 5, 2, 6, 1, 7, 0):
            for de in range(2):
                ty, te = (y + dy) % 8, (core + de) % 2
                src = pieces.at[half, ty, te]
                if dy or de:
                    start(src, dst, spread_send.at[half, dy * 2 + de], spread_recv.at[half], (x, z, ty, te))
                else:
                    pltpu.make_async_copy(src, dst, spread_recv.at[half]).start()

    def spread_x(half):
        for dx in range(4):
            tx = (x + dx) % 4
            src = rows_here.at[half, :, pl.ds(pl.multiple_of(32 * tx, 32), 32), :]
            dst = right_all.at[z, half, x]
            if dx:
                start(src, dst, third_send.at[half, dx], third_recv.at[half], (tx, z, y, core))
            else:
                pltpu.make_async_copy(src, dst, third_recv.at[half]).start()

    goes = (x1 != zh).astype(jnp.int32)
    for dx in range(4):
        tx = (x + dx) % 4
        dst = stage.at[goes, x0]
        if dx:
            start(packed.at[tx], dst, pack_send.at[dx], pack_recv.at[goes, x0], (tx, z, y, core))
        else:
            pltpu.make_async_copy(packed.at[tx], dst, pack_recv.at[goes, x0]).start()
    spread(0)
    spread(1)
    for f in range(2):
        arrive(stage.at[1, f], pack_recv.at[1, f])
        start(stage.at[1, f], far.at[f], far_send.at[f], far_recv.at[f], (x, (z + 4) % 8, y, core))

    for half in range(2):
        arrive(rows_here.at[half], spread_recv.at[half])
        spread_x(half)

    yr, yl, zr, zlft = (y + 1) % RING, (y + 7) % RING, (z + 1) % RING, (z + 7) % RING

    def send_y(slot, h, way, step):
        ref = left_all.at[slot, core, h]
        start(ref, ref, ysend.at[way, step, h], yrecv.at[way, step, h], (x, z, yr if way == 0 else yl, core))

    def send_z(slot, h, way, step):
        ref = right_all.at[slot, h]
        start(ref, ref, zsend.at[way, step, h], zrecv.at[way, step, h], (x, zr if way == 0 else zlft, y, core))

    def share(slot, h, number):
        ref = left_all.at[slot, core, h]
        start(ref, ref, share_send.at[number], share_recv.at[number], (x, z, y, 1 - core))

    def split_left(slot, e, h):
        lanes = pl.ds(pl.multiple_of(128 * e, 128), 128)
        left_hi[slot, h, :, lanes], left_lo[slot, h, :, lanes] = split(left_all[slot, e, h])

    def split_right(slot, half):
        high, low = split(right_all[slot, half])
        for s3 in range(2):
            for s2 in range(2):
                for k in range(2):
                    begin = pl.multiple_of(128 * k + 64 * s3 + 32 * (slot // 4), 32)
                    at = (s2 * 4 + slot % 4, pl.ds(begin, 32), slice(128 * half, 128 * half + 128))
                    right_hi[at] = high[2 * s3 + s2, k]
                    right_lo[at] = low[2 * s3 + s2, k]

    def ring_z_begin(h):
        arrive(right_all.at[z, h], third_recv.at[h])
        send_z(z, h, h, 0)
        send_z(z, h, 1 - h, 0)

    ring_z_begin(0)
    low_lane = lax.broadcasted_iota(jnp.int32, (128, 128), 1) < 64
    for f in range(2):
        arrive(stage.at[0, f], pack_recv.at[0, f])
        arrive(far.at[f], far_recv.at[f])
        near_part, far_part = stage[0, f], far[f]
        even = jnp.where(zh == 0, near_part, far_part)
        odd = jnp.where(zh == 0, far_part, near_part)
        left_all[y, core, f, 0:128] = jnp.where(low_lane, even, odd)
        left_all[y, core, f, 128:256] = pltpu.roll(jnp.where(low_lane, odd, even), 64, 1)
        send_y(y, f, f, 0)
        send_y(y, f, 1 - f, 0)
        share(y, f, f)
    ring_z_begin(1)
    shared = [(y, 0), (y, 1)]
    for h in range(2):
        split_right(z, h)
        split_left(y, core, h)
    for step in range(4):
        for i in range(2):
            for way in range(2):
                h = i if way == 0 else 1 - i
                if step == 3 and i == 1:
                    continue
                last = step == 3 or (step == 2 and i == 1)
                slot = (z - 1 - step + 8) % 8 if way == 0 else (z + 1 + step) % 8
                arrive(right_all.at[slot, h], zrecv.at[way, step, h])
                if not last:
                    send_z(slot, h, way, step + 1)
                slot_y = (y - 1 - step + 8) % 8 if way == 0 else (y + 1 + step) % 8
                arrive(left_all.at[slot_y, core, h], yrecv.at[way, step, h])
                if not last:
                    send_y(slot_y, h, way, step + 1)
                share(slot_y, h, len(shared))
                shared.append((slot_y, h))
                split_right(slot, h)
                split_left(slot_y, core, h)
    def take_shared(number):
        slot_y, h = shared[number]
        arrive(left_all.at[slot_y, 1 - core, h], share_recv.at[number])
        split_left(slot_y, 1 - core, h)

    def product(unit, f):
        lh, ll, rh, rl = left_hi[unit, f], left_lo[unit, f], right_hi[unit], right_lo[unit]
        return dot(lh, rh) + dot(lh, rl) + dot(ll, rh)

    for number in range(14):
        take_shared(number)
    for f in range(2):
        total = product((y + 5) % 8, f)
        for step in range(6, 12):
            total += product((y + step) % 8, f)
        for half in range(2):
            partial[f, half] = total[:, 128 * half : 128 * half + 128]
    for f in range(2):
        take_shared(14 + f)
        total = product((y + 4) % 8, f)
        for half in range(2):
            partial[f, half] += total[:, 128 * half : 128 * half + 128]
        for dx in (2, 1, 3):
            tx = (x + dx) % 4
            src = partial.at[f, :, pl.ds(pl.multiple_of(64 * tx, 64), 64), :]
            start(src, arrived.at[dx - 1, f], part_send.at[dx - 1, f], part_recv.at[dx - 1, f], (tx, z, y, core))

    for f in range(2):
        for d in range(3):
            arrive(arrived.at[d, f], part_recv.at[d, f])
        kept = partial[f, :, pl.ds(pl.multiple_of(64 * x, 64), 64), :]
        summed[f] = kept + arrived[0, f] + arrived[1, f] + arrived[2, f]
        for half in range(2):
            to = (2 * half + y // 4, zh * 4 + y % 4, 4 * f + zl, x // 2)
            dst = mirror.at[core, pl.ds(pl.multiple_of(64 * x0, 64), 64)]
            home = (to[0] == x) & (to[1] == z) & (to[2] == y) & (to[3] == core)
            start_or_keep(home, summed.at[f, half], dst, mirror_send.at[f, half], mirror_recv, to)
        for half in range(2):
            to = (2 * zh + f, half * 4 + zl, y, core)
            dst = own.at[pl.ds(pl.multiple_of(64 * x, 64), 64)]
            home = (to[0] == x) & (to[1] == z)
            start_or_keep(home, summed.at[f, half], dst, own_send.at[f, half], own_recv, to)

    arrive(own, own_recv)
    arrive(mirror, mirror_recv)
    for e in range(2):
        out_ref[128 * e : 128 * e + 128, :] = own[128 * e : 128 * e + 128] + jnp.transpose(mirror[e])

    for made in sends:
        made.wait_send()
    for home, made in maybe:
        pl.when(jnp.logical_not(home))(made.wait_send)


def body(integrals, amplitudes):
    dma = pltpu.SemaphoreType.DMA
    return pl.pallas_call(
        kernel,
        out_shape=jax.ShapeDtypeStruct((256, 128), F32),
        in_specs=[pl.BlockSpec(memory_space=pltpu.VMEM), pl.BlockSpec(memory_space=pltpu.VMEM)],
        out_specs=pl.BlockSpec(memory_space=pltpu.VMEM),
        scratch_shapes=[
            pltpu.VMEM((4, 128, 128), F32),
            pltpu.VMEM((2, 2, 128, 128), F32),
            pltpu.VMEM((2, 128, 128), F32),
            pltpu.VMEM((8, 2, 2, 256, 128), F32),
            pltpu.VMEM((2, 8, 2, 2, 8, 128), F32),
            pltpu.VMEM((2, 2, 128, 128), F32),
            pltpu.VMEM((8, 2, 4, 2, 32, 128), F32),
            pltpu.VMEM((8, 2, 256, 256), BF16),
            pltpu.VMEM((8, 2, 256, 256), BF16),
            pltpu.VMEM((8, 256, 256), BF16),
            pltpu.VMEM((8, 256, 256), BF16),
            pltpu.VMEM((2, 2, 256, 128), F32),
            pltpu.VMEM((3, 2, 2, 64, 128), F32),
            pltpu.VMEM((2, 2, 64, 128), F32),
            pltpu.VMEM((256, 128), F32),
            pltpu.VMEM((2, 128, 128), F32),
            dma((4,)), dma((2, 2)),
            dma((2,)), dma((2,)),
            dma((2, 16)), dma((2,)),
            dma((2, 4)), dma((2,)),
            dma((2, 4, 2)), dma((2, 4, 2)),
            dma((2, 4, 2)), dma((2, 4, 2)),
            dma((16,)), dma((16,)),
            dma((3, 2)), dma((3, 2)),
            dma((2, 2)), dma,
            dma((2, 2)), dma,
        ],
        compiler_params=pltpu.CompilerParams(
            collective_id=0, has_side_effects=True, vmem_limit_bytes=40 << 20
        ),
        cost_estimate=pl.CostEstimate(flops=3 * 2**29, bytes_accessed=1 << 20, transcendentals=0),
        name="cycle",
    )(integrals.reshape(512, 128), amplitudes)


def solution(mesh):
    return jax.shard_map(
        body,
        mesh=mesh,
        in_specs=(P("row", None, "col", None), P("row", "col", None, None)),
        out_specs=P("row", "col"),
        check_vma=False,
    )
```

```python
import jax
import jax.numpy as jnp
from jax import lax
from jax.experimental import pallas as pl
from jax.experimental.pallas import tpu as pltpu
from jax.sharding import PartitionSpec as P

MESH = pl.DeviceIdType.MESH
RING = 8
F32, BF16 = jnp.float32, jnp.bfloat16


def device(x, z, y, core):
    return (x * 4 + z % 4, (z // 4) * 16 + y * 2 + core)


def split(value):
    high = value.astype(BF16)
    return high, (value - high.astype(F32)).astype(BF16)


def dot(first, second):
    return jnp.dot(first, second, preferred_element_type=F32)


def kernel(
    left_ref, right_ref, out_ref,
    packed, stage, far, left_all, pieces, rows_here, right_all, left_hi, left_lo, right_hi, right_lo,
    partial, arrived, summed, own, mirror,
    pack_send, pack_recv, far_send, far_recv, spread_send, spread_recv, third_send, third_recv,
    ysend, yrecv, zsend, zrecv, share_send, share_recv,
    part_send, part_recv, own_send, own_recv, mirror_send, mirror_recv,
):
    row, col = lax.axis_index("row"), lax.axis_index("col")
    x, zl, zh, y, core = row // 4, row % 4, col // 16, (col // 2) % 8, col % 2
    z = zh * 4 + zl
    x1, x0 = x // 2, x % 2

    barrier = pltpu.get_barrier_semaphore()

    def greet(*target):
        pl.semaphore_signal(barrier, inc=1, device_id=device(*target), device_id_type=MESH)

    for dx in range(1, 4):
        greet((x + dx) % 4, z, y, core)
    for dz in (1, 7, 4):
        greet(x, (z + dz) % 8, y, core)
    for dy in range(8):
        for de in range(2):
            if dy or de:
                greet(x, z, (y + dy) % 8, (core + de) % 2)

    for half in range(2):
        for k in range(2):
            for e in range(2):
                block = right_ref[k, :, 8 * half : 8 * half + 8, 128 * e : 128 * e + 128]
                block = jnp.swapaxes(block, 0, 1)
                for j in range(8):
                    pieces[half, j, e, k] = block[j]

    lane = lax.broadcasted_iota(jnp.int32, (128, 128), 1)
    strips = []
    for i in range(2):
        for lanes in range(2):
            begin = 256 * (zh if i == 0 else 1 - zh) + lanes
            strips.append(left_ref[pl.ds(begin, 128, stride=2), :])
    for q in range(4):
        turned = [pltpu.roll(strip, (32 * i - 32 * q) % 128, 1) if i != q else strip for i, strip in enumerate(strips)]
        packed[q] = jnp.where(
            lane < 64,
            jnp.where(lane < 32, turned[0], turned[1]),
            jnp.where(lane < 96, turned[2], turned[3]),
        )

    pl.semaphore_wait(barrier, 21)

    sends = []
    maybe = []

    def copy(src, dst, send_sem, recv_sem, target):
        return pltpu.make_async_remote_copy(
            src_ref=src, dst_ref=dst, send_sem=send_sem, recv_sem=recv_sem,
            device_id=device(*target), device_id_type=MESH,
        )

    def start(*args):
        made = copy(*args)
        made.start()
        sends.append(made)

    def start_or_keep(home, src, dst, send_sem, recv_sem, target):
        made = copy(src, dst, send_sem, recv_sem, target)

        @pl.when(home)
        def _():
            pltpu.make_async_copy(src, dst, recv_sem).start()

        @pl.when(jnp.logical_not(home))
        def _():
            made.start()

        maybe.append((home, made))

    def arrive(ref, sem):
        pltpu.make_async_copy(ref, ref, sem).wait()

    def spread(half):
        mine = pl.ds(pl.multiple_of(16 * y + 8 * core, 8), 8)
        dst = rows_here.at[half, :, mine, :]
        for dy in (4, 3, 5, 2, 6, 1, 7, 0):
            for de in range(2):
                ty, te = (y + dy) % 8, (core + de) % 2
                src = pieces.at[half, ty, te]
                if dy or de:
                    start(src, dst, spread_send.at[half, dy * 2 + de], spread_recv.at[half], (x, z, ty, te))
                else:
                    pltpu.make_async_copy(src, dst, spread_recv.at[half]).start()

    def spread_x(half):
        for dx in range(4):
            tx = (x + dx) % 4
            src = rows_here.at[half, :, pl.ds(pl.multiple_of(32 * tx, 32), 32), :]
            dst = right_all.at[z, half, x]
            if dx:
                start(src, dst, third_send.at[half, dx], third_recv.at[half], (tx, z, y, core))
            else:
                pltpu.make_async_copy(src, dst, third_recv.at[half]).start()

    goes = (x1 != zh).astype(jnp.int32)
    for dx in range(4):
        tx = (x + dx) % 4
        dst = stage.at[goes, x0]
        if dx:
            start(packed.at[tx], dst, pack_send.at[dx], pack_recv.at[goes, x0], (tx, z, y, core))
        else:
            pltpu.make_async_copy(packed.at[tx], dst, pack_recv.at[goes, x0]).start()
    spread(0)
    spread(1)
    for f in range(2):
        arrive(stage.at[1, f], pack_recv.at[1, f])
        start(stage.at[1, f], far.at[f], far_send.at[f], far_recv.at[f], (x, (z + 4) % 8, y, core))

    for half in range(2):
        arrive(rows_here.at[half], spread_recv.at[half])
        spread_x(half)

    yr, yl, zr, zlft = (y + 1) % RING, (y + 7) % RING, (z + 1) % RING, (z + 7) % RING

    def send_y(slot, h, way, step):
        ref = left_all.at[slot, core, h]
        start(ref, ref, ysend.at[way, step, h], yrecv.at[way, step, h], (x, z, yr if way == 0 else yl, core))

    def send_z(slot, h, way, step):
        ref = right_all.at[slot, h]
        start(ref, ref, zsend.at[way, step, h], zrecv.at[way, step, h], (x, zr if way == 0 else zlft, y, core))

    def share(slot, h, number):
        ref = left_all.at[slot, core, h]
        start(ref, ref, share_send.at[number], share_recv.at[number], (x, z, y, 1 - core))

    def split_left(slot, e, h):
        lanes = pl.ds(pl.multiple_of(128 * e, 128), 128)
        left_hi[slot, h, :, lanes], left_lo[slot, h, :, lanes] = split(left_all[slot, e, h])

    def split_right(slot, half):
        high, low = split(right_all[slot, half])
        for s3 in range(2):
            for s2 in range(2):
                for k in range(2):
                    begin = pl.multiple_of(128 * k + 64 * s3 + 32 * (slot // 4), 32)
                    at = (s2 * 4 + slot % 4, pl.ds(begin, 32), slice(128 * half, 128 * half + 128))
                    right_hi[at] = high[2 * s3 + s2, k]
                    right_lo[at] = low[2 * s3 + s2, k]

    def ring_z_begin(h):
        arrive(right_all.at[z, h], third_recv.at[h])
        send_z(z, h, h, 0)
        send_z(z, h, 1 - h, 0)

    ring_z_begin(0)
    low_lane = lane < 64
    for f in range(2):
        arrive(stage.at[0, f], pack_recv.at[0, f])
        arrive(far.at[f], far_recv.at[f])
        near_part, far_part = stage[0, f], far[f]
        even = jnp.where(zh == 0, near_part, far_part)
        odd = jnp.where(zh == 0, far_part, near_part)
        left_all[y, core, f, 0:128] = jnp.where(low_lane, even, odd)
        left_all[y, core, f, 128:256] = pltpu.roll(jnp.where(low_lane, odd, even), 64, 1)
        send_y(y, f, f, 0)
        send_y(y, f, 1 - f, 0)
        share(y, f, f)
    ring_z_begin(1)
    shared = [(y, 0), (y, 1)]
    for h in range(2):
        split_right(z, h)
        split_left(y, core, h)
    def take_shared(number):
        slot_y, h = shared[number]
        arrive(left_all.at[slot_y, 1 - core, h], share_recv.at[number])
        split_left(slot_y, 1 - core, h)

    for step in range(4):
        for i in range(2 if step < 3 else 1):
            last = step == 3 or (step == 2 and i == 1)
            come = []
            for way in range(2):
                h = i if way == 0 else 1 - i
                slot_y = (y - 1 - step + 8) % 8 if way == 0 else (y + 1 + step) % 8
                arrive(left_all.at[slot_y, core, h], yrecv.at[way, step, h])
                if not last:
                    send_y(slot_y, h, way, step + 1)
                share(slot_y, h, len(shared))
                shared.append((slot_y, h))
                slot = (z - 1 - step + 8) % 8 if way == 0 else (z + 1 + step) % 8
                arrive(right_all.at[slot, h], zrecv.at[way, step, h])
                if not last:
                    send_z(slot, h, way, step + 1)
                come.append((slot_y, slot, h))
            for slot_y, slot, h in come:
                split_left(slot_y, core, h)
                split_right(slot, h)
            if len(shared) > 4:
                take_shared(len(shared) - 6)
                take_shared(len(shared) - 5)

    def product(unit, f):
        lh, ll, rh, rl = left_hi[unit, f], left_lo[unit, f], right_hi[unit], right_lo[unit]
        return dot(lh, rh) + dot(lh, rl) + dot(ll, rh)

    for number in range(12, 14):
        take_shared(number)
    for f in range(2):
        total = product((y + 5) % 8, f)
        for step in range(6, 12):
            total += product((y + step) % 8, f)
        for half in range(2):
            partial[f, half] = total[:, 128 * half : 128 * half + 128]
    for f in range(2):
        take_shared(14 + f)
        total = product((y + 4) % 8, f)
        for half in range(2):
            partial[f, half] += total[:, 128 * half : 128 * half + 128]
        for dx in (2, 1, 3):
            tx = (x + dx) % 4
            src = partial.at[f, :, pl.ds(pl.multiple_of(64 * tx, 64), 64), :]
            start(src, arrived.at[dx - 1, f], part_send.at[dx - 1, f], part_recv.at[dx - 1, f], (tx, z, y, core))

    for f in range(2):
        for d in range(3):
            arrive(arrived.at[d, f], part_recv.at[d, f])
        kept = partial[f, :, pl.ds(pl.multiple_of(64 * x, 64), 64), :]
        summed[f] = kept + arrived[0, f] + arrived[1, f] + arrived[2, f]
        for half in range(2):
            to = (2 * half + y // 4, zh * 4 + y % 4, 4 * f + zl, x // 2)
            dst = mirror.at[core, pl.ds(pl.multiple_of(64 * x0, 64), 64)]
            home = (to[0] == x) & (to[1] == z) & (to[2] == y) & (to[3] == core)
            start_or_keep(home, summed.at[f, half], dst, mirror_send.at[f, half], mirror_recv, to)
        for half in range(2):
            to = (2 * zh + f, half * 4 + zl, y, core)
            dst = own.at[pl.ds(pl.multiple_of(64 * x, 64), 64)]
            home = (to[0] == x) & (to[1] == z)
            start_or_keep(home, summed.at[f, half], dst, own_send.at[f, half], own_recv, to)

    arrive(own, own_recv)
    arrive(mirror, mirror_recv)
    for e in range(2):
        out_ref[128 * e : 128 * e + 128, :] = own[128 * e : 128 * e + 128] + jnp.transpose(mirror[e])

    for made in sends:
        made.wait_send()
    for home, made in maybe:
        pl.when(jnp.logical_not(home))(made.wait_send)


def body(integrals, amplitudes):
    dma = pltpu.SemaphoreType.DMA
    return pl.pallas_call(
        kernel,
        out_shape=jax.ShapeDtypeStruct((256, 128), F32),
        in_specs=[pl.BlockSpec(memory_space=pltpu.VMEM), pl.BlockSpec(memory_space=pltpu.VMEM)],
        out_specs=pl.BlockSpec(memory_space=pltpu.VMEM),
        scratch_shapes=[
            pltpu.VMEM((4, 128, 128), F32),
            pltpu.VMEM((2, 2, 128, 128), F32),
            pltpu.VMEM((2, 128, 128), F32),
            pltpu.VMEM((8, 2, 2, 256, 128), F32),
            pltpu.VMEM((2, 8, 2, 2, 8, 128), F32),
            pltpu.VMEM((2, 2, 128, 128), F32),
            pltpu.VMEM((8, 2, 4, 2, 32, 128), F32),
            pltpu.VMEM((8, 2, 256, 256), BF16),
            pltpu.VMEM((8, 2, 256, 256), BF16),
            pltpu.VMEM((8, 256, 256), BF16),
            pltpu.VMEM((8, 256, 256), BF16),
            pltpu.VMEM((2, 2, 256, 128), F32),
            pltpu.VMEM((3, 2, 2, 64, 128), F32),
            pltpu.VMEM((2, 2, 64, 128), F32),
            pltpu.VMEM((256, 128), F32),
            pltpu.VMEM((2, 128, 128), F32),
            dma((4,)), dma((2, 2)),
            dma((2,)), dma((2,)),
            dma((2, 16)), dma((2,)),
            dma((2, 4)), dma((2,)),
            dma((2, 4, 2)), dma((2, 4, 2)),
            dma((2, 4, 2)), dma((2, 4, 2)),
            dma((16,)), dma((16,)),
            dma((3, 2)), dma((3, 2)),
            dma((2, 2)), dma,
            dma((2, 2)), dma,
        ],
        compiler_params=pltpu.CompilerParams(
            collective_id=0, has_side_effects=True, vmem_limit_bytes=40 << 20
        ),
        cost_estimate=pl.CostEstimate(flops=3 * 2**29, bytes_accessed=1 << 20, transcendentals=0),
        name="cycle",
    )(integrals.reshape(512, 128), amplitudes)


def solution(mesh):
    return jax.shard_map(
        body,
        mesh=mesh,
        in_specs=(P("row", None, "col", None), P("row", "col", None, None)),
        out_specs=P("row", "col"),
        check_vma=False,
    )
```

```python
import jax
import jax.numpy as jnp
from jax import lax
from jax.experimental import pallas as pl
from jax.experimental.pallas import tpu as pltpu
from jax.sharding import PartitionSpec as P

MESH = pl.DeviceIdType.MESH
RING = 8
F32, BF16 = jnp.float32, jnp.bfloat16


def device(x, z, y, core):
    return (x * 4 + z % 4, (z // 4) * 16 + y * 2 + core)


def split(value):
    high = value.astype(BF16)
    return high, (value - high.astype(F32)).astype(BF16)


def dot(first, second):
    return jnp.dot(first, second, preferred_element_type=F32)


def kernel(
    left_ref, right_ref, out_ref,
    packed, stage, far, left_all, pieces, rows_here, right_all, left_hi, left_lo, right_hi, right_lo,
    partial, arrived, summed, own, mirror,
    pack_send, pack_recv, far_send, far_recv, spread_send, spread_recv, third_send, third_recv,
    ysend, yrecv, zsend, zrecv, share_send, share_recv,
    part_send, part_recv, own_send, own_recv, mirror_send, mirror_recv,
):
    row, col = lax.axis_index("row"), lax.axis_index("col")
    x, zl, zh, y, core = row // 4, row % 4, col // 16, (col // 2) % 8, col % 2
    z = zh * 4 + zl
    x1, x0 = x // 2, x % 2

    barrier = pltpu.get_barrier_semaphore()

    def greet(*target):
        pl.semaphore_signal(barrier, inc=1, device_id=device(*target), device_id_type=MESH)

    for dx in range(1, 4):
        greet((x + dx) % 4, z, y, core)
    for dz in (1, 7, 4):
        greet(x, (z + dz) % 8, y, core)
    for dy in range(8):
        for de in range(2):
            if dy or de:
                greet(x, z, (y + dy) % 8, (core + de) % 2)

    for half in range(2):
        for k in range(2):
            for e in range(2):
                block = right_ref[k, :, 8 * half : 8 * half + 8, 128 * e : 128 * e + 128]
                block = jnp.swapaxes(block, 0, 1)
                for j in range(8):
                    pieces[half, j, e, k] = block[j]

    lane = lax.broadcasted_iota(jnp.int32, (128, 128), 1)
    strips = []
    for i in range(2):
        for lanes in range(2):
            begin = pl.multiple_of(128 * (zh if i == 0 else 1 - zh), 128)
            strips.append(left_ref[pl.ds(begin, 128), 128 * lanes : 128 * lanes + 128])
    for q in range(4):
        turned = [pltpu.roll(strip, (32 * i - 32 * q) % 128, 1) if i != q else strip for i, strip in enumerate(strips)]
        packed[q] = jnp.where(
            lane < 64,
            jnp.where(lane < 32, turned[0], turned[1]),
            jnp.where(lane < 96, turned[2], turned[3]),
        )

    pl.semaphore_wait(barrier, 21)

    sends = []
    maybe = []

    def copy(src, dst, send_sem, recv_sem, target):
        return pltpu.make_async_remote_copy(
            src_ref=src, dst_ref=dst, send_sem=send_sem, recv_sem=recv_sem,
            device_id=device(*target), device_id_type=MESH,
        )

    def start(*args):
        made = copy(*args)
        made.start()
        sends.append(made)

    def start_or_keep(home, src, dst, send_sem, recv_sem, target):
        made = copy(src, dst, send_sem, recv_sem, target)

        @pl.when(home)
        def _():
            pltpu.make_async_copy(src, dst, recv_sem).start()

        @pl.when(jnp.logical_not(home))
        def _():
            made.start()

        maybe.append((home, made))

    def arrive(ref, sem):
        pltpu.make_async_copy(ref, ref, sem).wait()

    def spread(half):
        mine = pl.ds(pl.multiple_of(16 * y + 8 * core, 8), 8)
        dst = rows_here.at[half, :, mine, :]
        for dy in (4, 3, 5, 2, 6, 1, 7, 0):
            for de in range(2):
                ty, te = (y + dy) % 8, (core + de) % 2
                src = pieces.at[half, ty, te]
                if dy or de:
                    start(src, dst, spread_send.at[half, dy * 2 + de], spread_recv.at[half], (x, z, ty, te))
                else:
                    pltpu.make_async_copy(src, dst, spread_recv.at[half]).start()

    def spread_x(half):
        for dx in range(4):
            tx = (x + dx) % 4
            src = rows_here.at[half, :, pl.ds(pl.multiple_of(32 * tx, 32), 32), :]
            dst = right_all.at[z, half, x]
            if dx:
                start(src, dst, third_send.at[half, dx], third_recv.at[half], (tx, z, y, core))
            else:
                pltpu.make_async_copy(src, dst, third_recv.at[half]).start()

    goes = (x1 != zh).astype(jnp.int32)
    for dx in range(4):
        tx = (x + dx) % 4
        dst = stage.at[goes, x0]
        if dx:
            start(packed.at[tx], dst, pack_send.at[dx], pack_recv.at[goes, x0], (tx, z, y, core))
        else:
            pltpu.make_async_copy(packed.at[tx], dst, pack_recv.at[goes, x0]).start()
    spread(0)
    spread(1)
    for f in range(2):
        arrive(stage.at[1, f], pack_recv.at[1, f])
        start(stage.at[1, f], far.at[f], far_send.at[f], far_recv.at[f], (x, (z + 4) % 8, y, core))

    for half in range(2):
        arrive(rows_here.at[half], spread_recv.at[half])
        spread_x(half)

    yr, yl, zr, zlft = (y + 1) % RING, (y + 7) % RING, (z + 1) % RING, (z + 7) % RING

    def send_y(slot, h, way, step):
        ref = left_all.at[slot, core, h]
        start(ref, ref, ysend.at[way, step, h], yrecv.at[way, step, h], (x, z, yr if way == 0 else yl, core))

    def send_z(slot, h, way, step):
        ref = right_all.at[slot, h]
        start(ref, ref, zsend.at[way, step, h], zrecv.at[way, step, h], (x, zr if way == 0 else zlft, y, core))

    def share(slot, h, number):
        ref = left_all.at[slot, core, h]
        start(ref, ref, share_send.at[number], share_recv.at[number], (x, z, y, 1 - core))

    def split_left(slot, e, h):
        lanes = pl.ds(pl.multiple_of(128 * e, 128), 128)
        left_hi[slot, h, :, lanes], left_lo[slot, h, :, lanes] = split(left_all[slot, e, h])

    def split_right(slot, half):
        high, low = split(right_all[slot, half])
        for s3 in range(2):
            for s2 in range(2):
                for k in range(2):
                    begin = pl.multiple_of(128 * k + 64 * s3 + 32 * (slot // 4), 32)
                    at = (s2 * 4 + slot % 4, pl.ds(begin, 32), slice(128 * half, 128 * half + 128))
                    right_hi[at] = high[2 * s3 + s2, k]
                    right_lo[at] = low[2 * s3 + s2, k]

    def ring_z_begin(h):
        arrive(right_all.at[z, h], third_recv.at[h])
        send_z(z, h, h, 0)
        send_z(z, h, 1 - h, 0)

    ring_z_begin(0)
    low_lane = lane < 64
    for f in range(2):
        arrive(stage.at[0, f], pack_recv.at[0, f])
        arrive(far.at[f], far_recv.at[f])
        near_part, far_part = stage[0, f], far[f]
        even = jnp.where(zh == 0, near_part, far_part)
        odd = jnp.where(zh == 0, far_part, near_part)
        left_all[y, core, f, 0:128] = jnp.where(low_lane, even, odd)
        left_all[y, core, f, 128:256] = pltpu.roll(jnp.where(low_lane, odd, even), 64, 1)
        send_y(y, f, f, 0)
        send_y(y, f, 1 - f, 0)
        share(y, f, f)
    ring_z_begin(1)
    shared = [(y, 0), (y, 1)]
    for h in range(2):
        split_right(z, h)
        split_left(y, core, h)
    def take_shared(number):
        slot_y, h = shared[number]
        arrive(left_all.at[slot_y, 1 - core, h], share_recv.at[number])
        split_left(slot_y, 1 - core, h)

    for step in range(4):
        for i in range(2 if step < 3 else 1):
            last = step == 3 or (step == 2 and i == 1)
            come = []
            for way in range(2):
                h = i if way == 0 else 1 - i
                slot_y = (y - 1 - step + 8) % 8 if way == 0 else (y + 1 + step) % 8
                arrive(left_all.at[slot_y, core, h], yrecv.at[way, step, h])
                if not last:
                    send_y(slot_y, h, way, step + 1)
                share(slot_y, h, len(shared))
                shared.append((slot_y, h))
                slot = (z - 1 - step + 8) % 8 if way == 0 else (z + 1 + step) % 8
                arrive(right_all.at[slot, h], zrecv.at[way, step, h])
                if not last:
                    send_z(slot, h, way, step + 1)
                come.append((slot_y, slot, h))
            for slot_y, slot, h in come:
                split_left(slot_y, core, h)
                split_right(slot, h)
            if len(shared) > 4:
                take_shared(len(shared) - 6)
                take_shared(len(shared) - 5)

    def product(unit, f):
        lh, ll, rh, rl = left_hi[unit, f], left_lo[unit, f], right_hi[unit], right_lo[unit]
        return dot(lh, rh) + dot(lh, rl) + dot(ll, rh)

    for number in range(12, 14):
        take_shared(number)
    for f in range(2):
        total = product((y + 5) % 8, f)
        for step in range(6, 12):
            total += product((y + step) % 8, f)
        for half in range(2):
            partial[f, half] = total[:, 128 * half : 128 * half + 128]
    for f in range(2):
        take_shared(14 + f)
        total = product((y + 4) % 8, f)
        for half in range(2):
            partial[f, half] += total[:, 128 * half : 128 * half + 128]
        for dx in (2, 1, 3):
            tx = (x + dx) % 4
            src = partial.at[f, :, pl.ds(pl.multiple_of(64 * tx, 64), 64), :]
            start(src, arrived.at[dx - 1, f], part_send.at[dx - 1, f], part_recv.at[dx - 1, f], (tx, z, y, core))

    for f in range(2):
        for d in range(3):
            arrive(arrived.at[d, f], part_recv.at[d, f])
        kept = partial[f, :, pl.ds(pl.multiple_of(64 * x, 64), 64), :]
        summed[f] = kept + arrived[0, f] + arrived[1, f] + arrived[2, f]
        for half in range(2):
            to = (2 * half + y // 4, zh * 4 + y % 4, 4 * f + zl, x // 2)
            dst = mirror.at[core, pl.ds(pl.multiple_of(64 * x0, 64), 64)]
            home = (to[0] == x) & (to[1] == z) & (to[2] == y) & (to[3] == core)
            start_or_keep(home, summed.at[f, half], dst, mirror_send.at[f, half], mirror_recv, to)
        for half in range(2):
            to = (2 * zh + f, half * 4 + zl, y, core)
            dst = own.at[pl.ds(pl.multiple_of(64 * x, 64), 64)]
            home = (to[0] == x) & (to[1] == z)
            start_or_keep(home, summed.at[f, half], dst, own_send.at[f, half], own_recv, to)

    arrive(own, own_recv)
    arrive(mirror, mirror_recv)
    for e in range(2):
        out_ref[128 * e : 128 * e + 128, :] = own[128 * e : 128 * e + 128] + jnp.transpose(mirror[e])

    for made in sends:
        made.wait_send()
    for home, made in maybe:
        pl.when(jnp.logical_not(home))(made.wait_send)


def body(integrals, amplitudes):
    dma = pltpu.SemaphoreType.DMA
    return pl.pallas_call(
        kernel,
        out_shape=jax.ShapeDtypeStruct((256, 128), F32),
        in_specs=[pl.BlockSpec(memory_space=pltpu.VMEM), pl.BlockSpec(memory_space=pltpu.VMEM)],
        out_specs=pl.BlockSpec(memory_space=pltpu.VMEM),
        scratch_shapes=[
            pltpu.VMEM((4, 128, 128), F32),
            pltpu.VMEM((2, 2, 128, 128), F32),
            pltpu.VMEM((2, 128, 128), F32),
            pltpu.VMEM((8, 2, 2, 256, 128), F32),
            pltpu.VMEM((2, 8, 2, 2, 8, 128), F32),
            pltpu.VMEM((2, 2, 128, 128), F32),
            pltpu.VMEM((8, 2, 4, 2, 32, 128), F32),
            pltpu.VMEM((8, 2, 256, 256), BF16),
            pltpu.VMEM((8, 2, 256, 256), BF16),
            pltpu.VMEM((8, 256, 256), BF16),
            pltpu.VMEM((8, 256, 256), BF16),
            pltpu.VMEM((2, 2, 256, 128), F32),
            pltpu.VMEM((3, 2, 2, 64, 128), F32),
            pltpu.VMEM((2, 2, 64, 128), F32),
            pltpu.VMEM((256, 128), F32),
            pltpu.VMEM((2, 128, 128), F32),
            dma((4,)), dma((2, 2)),
            dma((2,)), dma((2,)),
            dma((2, 16)), dma((2,)),
            dma((2, 4)), dma((2,)),
            dma((2, 4, 2)), dma((2, 4, 2)),
            dma((2, 4, 2)), dma((2, 4, 2)),
            dma((16,)), dma((16,)),
            dma((3, 2)), dma((3, 2)),
            dma((2, 2)), dma,
            dma((2, 2)), dma,
        ],
        compiler_params=pltpu.CompilerParams(
            collective_id=0, has_side_effects=True, vmem_limit_bytes=40 << 20
        ),
        cost_estimate=pl.CostEstimate(flops=3 * 2**29, bytes_accessed=1 << 20, transcendentals=0),
        name="cycle",
    )(integrals.reshape(256, 256), amplitudes)


def solution(mesh):
    return jax.shard_map(
        body,
        mesh=mesh,
        in_specs=(P("row", None, "col", None), P("row", "col", None, None)),
        out_specs=P("row", "col"),
        check_vma=False,
    )
```
